32 devices in a mesh: ens: 2 (over y), tile: 16 (over z, x, core).
Axes of the slice: x: 2, y: 2, z: 4, core: 2. Of those that a mesh axis runs over, the one named last changes fastest.
Arguments:
- ocean_state: bfloat16 [512, 512, 128], P(('ens', 'tile')), parts along dimension 0, may hold values from -6 to 6
- atm_flux: bfloat16 [8, 16384], P(None, ('ens', 'tile')), parts along dimension 1, may hold values from -6 to 6
- lat_weights: float32 [256, 6], P('tile'), may hold values from -2.5 to 2.5
- lon_weights: bfloat16 [128, 512], replicated, may hold values from -0.5 to 0.5
- flux_proj: bfloat16 [8, 128], replicated, may hold values from -2 to 2
- conv_kernel: bfloat16 [2, 9, 128, 128], replicated, may hold values from -0.1875 to 0.1875
- conv_bias: float32 [2, 128], replicated, may hold values from -3 to 3
- head: bfloat16 [128, 4], replicated, may hold values from -0.5 to 0.5
Outputs:
- ocean_next: bfloat16 [512, 512, 128], P(('ens', 'tile')), parts along dimension 0
- fields: float32 [4, 512, 512], P(None, ('ens', 'tile')), parts along dimension 1
The draws below stay inside these ranges and needn't reach their ends.
There are 2 independent parts, one for each index of `ens`. The reference program is written for one: setup_inputs(seed, part) draws one part's arguments, and reference() takes and returns one part's arrays. A program takes and returns all parts, laid end to end along the dimension named above; an argument that names none is the same for every part. Nothing has to cross between parts.
All inputs are finite; a program needn't handle non-finite values.
Results may differ from the reference program's by a relative error of at most 0.0064.
Values may be sent and summed in bfloat16 or wider, within the bound.
A program may use at most 64 MiB of HBM per device.

```python
import jax
import jax.numpy as jnp
import numpy as np
from jax import lax

CHANNELS = 128
FLUXES = 8
FIELDS = 4
LAYERS = 2
OR_DEV = 16
OCW = 512
AL_DEV = 4
NR = 256
AL = 64
ALON = 128
N_TILE = 16


def steps_of(rng, shape, split, least, high):
    gain = 1.0
    for position, shards_of in split:
        steps = jax.random.uniform(jax.random.fold_in(jax.random.fold_in(rng, 6), position), (shards_of,), jnp.float32, least / len(split), high / len(split))
        gain = gain * jnp.repeat(jnp.exp(steps), shape[position] // shards_of).reshape((-1,) + (1,) * (len(shape) - 1 - position))
    return gain


def bell_draw(key, dims, width, bound, cuts=(), dtype=jnp.bfloat16):
    level = steps_of(key, dims, cuts, -0.22, 0.18) if cuts else 1.0
    values = jax.random.normal(key, dims, jnp.float32) * width * level
    return jnp.minimum(jnp.maximum(values, -bound), bound).astype(dtype)


def setup_inputs(seed: int = 0, part: int = 0) -> dict:
    seeds = jax.random.split(jax.random.key(seed), 9)
    part_keys = jax.random.split(jax.random.fold_in(seeds[8], part), 9)
    return {
        "ocean_state": bell_draw(part_keys[0], (NR, OCW, CHANNELS), 1.0, 6.0, ((0, 16),)),
        "atm_flux": bell_draw(part_keys[1], (FLUXES, ALON * AL), 1.0, 6.0, ((1, 16),)),
        "lat_weights": bell_draw(seeds[2], (NR, AL_DEV + 2), (AL_DEV + 2) ** -0.5, 2.5, ((0, 16),), jnp.float32),
        "lon_weights": bell_draw(seeds[3], (ALON, OCW), ALON ** -0.5, 0.5),
        "flux_proj": bell_draw(seeds[4], (FLUXES, CHANNELS), FLUXES ** -0.5, 2.0),
        "conv_kernel": bell_draw(seeds[5], (LAYERS, 9, CHANNELS, CHANNELS), (9 * CHANNELS) ** -0.5, 0.1875),
        "conv_bias": bell_draw(seeds[6], (LAYERS, CHANNELS), 0.5, 3.0, (), jnp.float32),
        "head": bell_draw(seeds[7], (CHANNELS, FIELDS), CHANNELS ** -0.5, 0.5),
    }


def conv_layer(state, kernel, bias):
    padded = jnp.pad(state, ((1, 1), (0, 0), (0, 0)))
    total = jnp.zeros((NR * OCW, CHANNELS), jnp.float32)
    for offset in range(3):
        band = padded[offset:offset + NR]
        stacked = jnp.concatenate([jnp.roll(band, 1 - shift_col, axis=1) for shift_col in range(3)], axis=2)
        taps = kernel[3 * offset:3 * offset + 3].reshape(3 * CHANNELS, CHANNELS)
        total = total + jnp.dot(stacked.reshape(NR * OCW, 3 * CHANNELS), taps, preferred_element_type=jnp.float32)
    hidden = total.reshape(NR, OCW, CHANNELS) + bias
    return (state.astype(jnp.float32) + jax.nn.gelu(hidden, approximate=False)).astype(jnp.bfloat16)


def reference(ocean_state, atm_flux, lat_weights, lon_weights, flux_proj, conv_kernel, conv_bias, head):
    cells = atm_flux.reshape(FLUXES, ALON, AL)
    padded = jnp.pad(cells, ((0, 0), (0, 0), (1, 1)))
    index = np.arange(N_TILE)[:, None] * AL_DEV + np.arange(AL_DEV + 2)[None, :]
    window = padded[:, :, index].astype(jnp.float32)
    across = jnp.einsum('flia,lc->fiac', window, lon_weights.astype(jnp.float32), precision=lax.Precision.HIGHEST)
    lat_block = lat_weights.reshape(N_TILE, OR_DEV, AL_DEV + 2)
    mapped = jnp.einsum('fiac,ira->firc', across, lat_block, precision=lax.Precision.HIGHEST)
    mapped = mapped.reshape(FLUXES, NR, OCW).astype(jnp.bfloat16)
    forcing = jnp.einsum('frc,fk->rck', mapped.astype(jnp.float32), flux_proj.astype(jnp.float32))
    state = (ocean_state.astype(jnp.float32) + forcing).astype(jnp.bfloat16)
    for layer in range(LAYERS):
        state = conv_layer(state, conv_kernel[layer], conv_bias[layer])
    fields = jnp.einsum('rck,kj->jrc', state.astype(jnp.float32), head.astype(jnp.float32))
    return state, fields
```

```python
import functools

import jax
import jax.numpy as jnp
from jax import lax
from jax.experimental import pallas as pl
from jax.experimental.pallas import tpu as pltpu
from jax.sharding import PartitionSpec as P

MESH = pl.DeviceIdType.MESH
HALO = 2
WINDOW = 16
CHUNK = 256


def exchange_kernel(
    tiles, ocean, flux, lat_own, lon, q_out, halo_out,
    sectors, lat_near, send, recv, halo_send, halo_recv, lat_send, lat_recv,
):
    me = lax.axis_index("tile")
    rows, width, _ = ocean.shape
    nflux = flux.shape[0]
    nlon = lon.shape[0]
    per_dev = nlon // tiles
    nlat = flux.shape[1] // per_dev
    band = nlat // tiles
    taps = lat_own.shape[1]

    barrier = pltpu.get_barrier_semaphore()

    def greet(k, carry):
        pl.semaphore_signal(
            barrier, inc=1, device_id={"tile": lax.rem(me + k, tiles)}, device_id_type=MESH
        )
        return carry

    lax.fori_loop(1, tiles, greet, 0)
    pl.semaphore_wait(barrier, tiles - 1)

    def flux_copy(slot, target, sem):
        return pltpu.make_async_remote_copy(
            src_ref=flux, dst_ref=sectors.at[slot], send_sem=send.at[sem], recv_sem=recv.at[slot],
            device_id={"tile": target}, device_id_type=MESH,
        )

    def lat_copy(slot, target):
        return pltpu.make_async_remote_copy(
            src_ref=lat_own, dst_ref=lat_near.at[slot], send_sem=lat_send.at[slot],
            recv_sem=lat_recv.at[slot], device_id={"tile": target}, device_id_type=MESH,
        )

    def halo_copy(slot, target):
        first = rows - HALO if slot == 0 else 0
        return pltpu.make_async_remote_copy(
            src_ref=ocean.at[pl.ds(first, HALO)], dst_ref=halo_out.at[pl.ds(slot * HALO, HALO)],
            send_sem=halo_send.at[slot], recv_sem=halo_recv.at[slot],
            device_id={"tile": target}, device_id_type=MESH,
        )

    after = lax.rem(me + 1, tiles)
    before = lax.rem(me + tiles - 1, tiles)

    def push(k, carry):
        flux_copy(me, lax.rem(me + k, tiles), k).start()
        return carry

    lax.fori_loop(1, tiles, push, 0)

    @pl.when(me < tiles - 1)
    def _():
        lat_copy(0, after).start()
        halo_copy(0, after).start()

    @pl.when(me > 0)
    def _():
        lat_copy(1, before).start()
        halo_copy(1, before).start()

    @pl.when(me == 0)
    def _():
        lat_near[0] = jnp.zeros_like(lat_own)

    @pl.when(me == tiles - 1)
    def _():
        lat_near[1] = jnp.zeros_like(lat_own)

    sectors[me] = flux[...]

    block = max(nlat, 128)
    group = block // nlat
    span = WINDOW * nflux
    low = me * band - band - 1
    row_id = lax.broadcasted_iota(jnp.int32, (span, block), 0)
    lane_id = lax.broadcasted_iota(jnp.int32, (span, block), 1)
    wanted = low + row_id // nflux
    picks = [
        ((lane_id == wanted + h * nlat) & (wanted >= 0) & (wanted < nlat))
        .astype(jnp.float32).astype(jnp.bfloat16)
        for h in range(group)
    ]
    pairs = tiles * nflux
    same_flux = (
        lax.broadcasted_iota(jnp.int32, (span, pairs), 0) % nflux
        == lax.broadcasted_iota(jnp.int32, (span, pairs), 1) % nflux
    )
    place_row = lax.broadcasted_iota(jnp.int32, (pairs, nlon), 0)
    place_lane = lax.broadcasted_iota(jnp.int32, (pairs, nlon), 1)

    def arrived(k, carry):
        source = lax.rem(me + k, tiles)
        flux_copy(source, source, k).wait_recv()
        return carry

    lax.fori_loop(1, tiles, arrived, 0)

    cells = jnp.zeros((span, nlon), jnp.float32)
    for number in range(per_dev):
        start = number // group * block
        piece = sectors[:, :, start : start + block].reshape(pairs, block)
        found = lax.dot_general(
            picks[number % group], piece, (((1,), (1,)), ((), ())),
            preferred_element_type=jnp.float32,
        )
        found = jnp.where(same_flux, found, 0.0).astype(jnp.bfloat16)
        place = (
            (place_lane == place_row // nflux * per_dev + number)
            .astype(jnp.float32).astype(jnp.bfloat16)
        )
        cells = cells + jnp.dot(found, place, preferred_element_type=jnp.float32)
    across = jnp.dot(
        cells.astype(jnp.bfloat16), lon[...], preferred_element_type=jnp.float32
    )

    @pl.when(me > 0)
    def _():
        lat_copy(0, before).wait_recv()

    @pl.when(me < tiles - 1)
    def _():
        lat_copy(1, after).wait_recv()

    weights = [(lat_near[0], rows - HALO + r, 0) for r in range(HALO)]
    weights += [(lat_own[...], r, band) for r in range(rows)]
    weights += [(lat_near[1], r, 2 * band) for r in range(HALO)]
    mapped = []
    for table, r, offset in weights:
        total = None
        for a in range(taps):
            level = (offset + a) * nflux
            term = table[r : r + 1, a : a + 1] * across[level : level + nflux]
            total = term if total is None else total + term
        mapped.append(total)
    q_out[...] = jnp.concatenate(mapped, axis=0).astype(jnp.bfloat16)

    @pl.when(me > 0)
    def _():
        halo_copy(0, before).wait_recv()
        halo_copy(1, before).wait_send()
        lat_copy(1, before).wait_send()

    @pl.when(me < tiles - 1)
    def _():
        halo_copy(1, after).wait_recv()
        halo_copy(0, after).wait_send()
        lat_copy(0, after).wait_send()

    def left(k, carry):
        flux_copy(me, lax.rem(me + k, tiles), k).wait_send()
        return carry

    lax.fori_loop(1, tiles, left, 0)


def gelu(y):
    return 0.5 * y * (1.0 + lax.erf(y * 0.7071067811865476))


def ocean_kernel(
    tiles, ocean, halo, q, proj, kernel, bias, head, next_out, fields_out,
    raw, state, hidden, taps, result, in_sem, out_sem,
):
    me = lax.axis_index("tile")
    rows, width, chans = ocean.shape
    nflux = proj.shape[0]
    layers = kernel.shape[0]
    pairs = rows // 2
    nfields = head.shape[0]
    wide = 3 * chans

    def fetch(p):
        return pltpu.make_async_copy(
            ocean.at[pl.ds(2 * p - 2, 2)], raw.at[pl.ds(2 * p, 2)], in_sem.at[p]
        )

    def fetch_halo(slot):
        p = slot * (pairs + 1)
        return pltpu.make_async_copy(
            halo.at[pl.ds(slot * HALO, HALO)], raw.at[pl.ds(2 * p, 2)], in_sem.at[p]
        )

    fetch_halo(0).start()
    for p in range(1, pairs + 1):
        fetch(p).start()
    fetch_halo(1).start()

    zero = jnp.zeros((chans, chans), jnp.bfloat16)
    for layer in range(layers):
        for i in range(4):
            for o in range(2):
                for dx in range(3):
                    dy = i - o
                    tap = kernel[layer, 3 * dy + dx] if 0 <= dy < 3 else zero
                    taps[
                        layer, i * wide + dx * chans : i * wide + (dx + 1) * chans,
                        o * chans : (o + 1) * chans,
                    ] = tap

    spread = jnp.concatenate([proj[...].astype(jnp.float32)] * 2, axis=0)
    spread = jnp.concatenate([spread] * 2, axis=1)
    spread = jnp.where(
        lax.broadcasted_iota(jnp.int32, spread.shape, 0) // nflux
        == lax.broadcasted_iota(jnp.int32, spread.shape, 1) // chans,
        spread, 0.0,
    ).astype(jnp.bfloat16)

    def put(ref, p, o, value):
        lane = o * wide
        ref[p, :, lane : lane + chans] = pltpu.roll(value, 1, 0).astype(jnp.bfloat16)
        ref[p, :, lane + 2 * chans : lane + wide] = pltpu.roll(value, width - 1, 0).astype(
            jnp.bfloat16
        )

    def force(p, carry):
        @pl.when(p == 0)
        def _():
            fetch_halo(0).wait()

        @pl.when(p == pairs + 1)
        def _():
            fetch_halo(1).wait()

        @pl.when((p > 0) & (p <= pairs))
        def _():
            fetch(p).wait()

        forcing = lax.dot_general(
            q[pl.ds(pl.multiple_of(p * 2 * nflux, 2 * nflux), 2 * nflux), :], spread,
            (((0,), (0,)), ((), ())), preferred_element_type=jnp.float32,
        )
        for o in range(2):
            u = raw[2 * p + o].astype(jnp.float32) + forcing[:, o * chans : (o + 1) * chans]
            u = u.astype(jnp.bfloat16)
            state[p, :, o * wide + chans : o * wide + 2 * chans] = u
            put(state, p, o, u.astype(jnp.float32))
        return carry

    lax.fori_loop(0, pairs + 2, force, 0)

    @pl.when(me == 0)
    def _():
        state[0] = jnp.zeros((width, 2 * wide), jnp.bfloat16)

    @pl.when(me == tiles - 1)
    def _():
        state[pairs + 1] = jnp.zeros((width, 2 * wide), jnp.bfloat16)

    def conv(source, j, layer, c):
        near = source[j, c : c + CHUNK, :]
        far = source[j + 1, c : c + CHUNK, :]
        y = jnp.dot(
            jnp.concatenate([near, far], axis=1), taps[layer], preferred_element_type=jnp.float32
        )
        b = bias[layer : layer + 1, :]
        g0 = gelu(y[:, :chans] + b)
        g1 = gelu(y[:, chans:] + b)
        v0 = near[:, wide + chans : wide + 2 * chans].astype(jnp.float32) + g0
        v1 = far[:, chans : 2 * chans].astype(jnp.float32) + g1
        return v0.astype(jnp.bfloat16), v1.astype(jnp.bfloat16)

    def first(j, carry):
        for c in range(0, width, CHUNK):
            v0, v1 = conv(state, j, 0, c)
            hidden[j, c : c + CHUNK, chans : 2 * chans] = v0
            hidden[j, c : c + CHUNK, wide + chans : wide + 2 * chans] = v1
        for o in range(2):
            lane = o * wide + chans
            put(hidden, j, o, hidden[j, :, lane : lane + chans].astype(jnp.float32))
        return carry

    lax.fori_loop(0, pairs + 1, first, 0)

    @pl.when(me == 0)
    def _():
        hidden[0, :, :wide] = jnp.zeros((width, wide), jnp.bfloat16)

    @pl.when(me == tiles - 1)
    def _():
        hidden[pairs, :, wide:] = jnp.zeros((width, wide), jnp.bfloat16)

    def store(m):
        return pltpu.make_async_copy(
            result.at[pl.ds(2 * m, 2)], next_out.at[pl.ds(2 * m, 2)], out_sem.at[m]
        )

    def second(m, carry):
        for c in range(0, width, CHUNK):
            for o, v in enumerate(conv(hidden, m, 1, c)):
                result[2 * m + o, c : c + CHUNK, :] = v
                fields_out[:, 2 * m + o, c : c + CHUNK] = lax.dot_general(
                    head[...], v, (((1,), (1,)), ((), ())), preferred_element_type=jnp.float32
                )
        store(m).start()
        return carry

    lax.fori_loop(0, pairs, second, 0)

    def finish(m, carry):
        store(m).wait()
        return carry

    lax.fori_loop(0, pairs, finish, 0)


def shards(
    ocean_state, atm_flux, lat_weights, lon_weights, flux_proj, conv_kernel, conv_bias, head
):
    rows, width, chans = ocean_state.shape
    tiles = lax.axis_size("tile")
    nflux = atm_flux.shape[0]
    vmem = pl.BlockSpec(memory_space=pltpu.VMEM)
    hbm = pl.BlockSpec(memory_space=pl.ANY)
    pair_sem = pltpu.SemaphoreType.DMA((2,))
    q, halo = pl.pallas_call(
        functools.partial(exchange_kernel, tiles),
        out_shape=(
            jax.ShapeDtypeStruct(((rows + 2 * HALO) * nflux, width), jnp.bfloat16),
            jax.ShapeDtypeStruct((2 * HALO, width, chans), jnp.bfloat16),
        ),
        in_specs=[hbm, vmem, vmem, vmem],
        out_specs=(vmem, hbm),
        scratch_shapes=[
            pltpu.VMEM((tiles,) + atm_flux.shape, jnp.bfloat16),
            pltpu.VMEM((2,) + lat_weights.shape, jnp.float32),
            pltpu.SemaphoreType.DMA((tiles,)),
            pltpu.SemaphoreType.DMA((tiles,)),
            pair_sem, pair_sem, pair_sem, pair_sem,
        ],
        compiler_params=pltpu.CompilerParams(
            collective_id=0, has_side_effects=True, vmem_limit_bytes=48 * 2**20
        ),
        name="exchange",
    )(ocean_state, atm_flux, lat_weights, lon_weights)
    pairs = rows // 2
    wide = 3 * chans
    return pl.pallas_call(
        functools.partial(ocean_kernel, tiles),
        out_shape=(
            jax.ShapeDtypeStruct(ocean_state.shape, jnp.bfloat16),
            jax.ShapeDtypeStruct((head.shape[1], rows, width), jnp.float32),
        ),
        in_specs=[hbm, hbm, vmem, vmem, vmem, vmem, vmem],
        out_specs=(hbm, vmem),
        scratch_shapes=[
            pltpu.VMEM((rows + 2 * HALO, width, chans), jnp.bfloat16),
            pltpu.VMEM((pairs + 2, width, 2 * wide), jnp.bfloat16),
            pltpu.VMEM((pairs + 1, width, 2 * wide), jnp.bfloat16),
            pltpu.VMEM((conv_kernel.shape[0], 4 * wide, 2 * chans), jnp.bfloat16),
            pltpu.VMEM(ocean_state.shape, jnp.bfloat16),
            pltpu.SemaphoreType.DMA((pairs + 2,)),
            pltpu.SemaphoreType.DMA((pairs,)),
        ],
        compiler_params=pltpu.CompilerParams(vmem_limit_bytes=48 * 2**20),
        name="ocean",
    )(ocean_state, halo, q, flux_proj, conv_kernel, conv_bias, head.T)


def solution(mesh):
    in_specs = (
        P(("ens", "tile"), None, None),
        P(None, ("ens", "tile")),
        P("tile", None),
        P(),
        P(),
        P(),
        P(),
        P(),
    )
    out_specs = (P(("ens", "tile"), None, None), P(None, ("ens", "tile"), None))
    return jax.shard_map(shards, mesh=mesh, in_specs=in_specs, out_specs=out_specs, check_vma=False)
```

```python
import functools

import jax
import jax.numpy as jnp
from jax import lax
from jax.experimental import pallas as pl
from jax.experimental.pallas import tpu as pltpu
from jax.sharding import PartitionSpec as P

MESH = pl.DeviceIdType.MESH
HALO = 2
WINDOW = 16


def exchange_kernel(
    tiles, ocean, flux, lat_in, lon_in, q_out, halo_out,
    sectors, lat_near, lat_own, lon, send, recv, halo_send, halo_recv, lat_send, lat_recv,
    local_sem,
):
    me = lax.axis_index("tile")
    rows, width, _ = ocean.shape
    nflux = flux.shape[0]
    nlon = lon_in.shape[0]
    per_dev = nlon // tiles
    nlat = flux.shape[1] // per_dev
    band = nlat // tiles
    taps = lat_in.shape[0]

    barrier = pltpu.get_barrier_semaphore()
    local = [
        pltpu.make_async_copy(flux, sectors.at[me], local_sem.at[0]),
        pltpu.make_async_copy(lat_in, lat_own, local_sem.at[1]),
        pltpu.make_async_copy(lon_in, lon, local_sem.at[2]),
    ]
    for copy in local:
        copy.start()

    def greet(k, carry):
        pl.semaphore_signal(
            barrier, inc=1, device_id={"tile": lax.rem(me + k, tiles)}, device_id_type=MESH
        )
        return carry

    lax.fori_loop(1, tiles, greet, 0)
    pl.semaphore_wait(barrier, tiles - 1)

    def flux_copy(slot, target, sem):
        return pltpu.make_async_remote_copy(
            src_ref=flux, dst_ref=sectors.at[slot], send_sem=send.at[sem], recv_sem=recv.at[slot],
            device_id={"tile": target}, device_id_type=MESH,
        )

    def lat_copy(slot, target):
        return pltpu.make_async_remote_copy(
            src_ref=lat_in, dst_ref=lat_near.at[slot], send_sem=lat_send.at[slot],
            recv_sem=lat_recv.at[slot], device_id={"tile": target}, device_id_type=MESH,
        )

    def halo_copy(slot, target):
        first = rows - HALO if slot == 0 else 0
        return pltpu.make_async_remote_copy(
            src_ref=ocean.at[pl.ds(first, HALO)], dst_ref=halo_out.at[pl.ds(slot * HALO, HALO)],
            send_sem=halo_send.at[slot], recv_sem=halo_recv.at[slot],
            device_id={"tile": target}, device_id_type=MESH,
        )

    after = lax.rem(me + 1, tiles)
    before = lax.rem(me + tiles - 1, tiles)

    def push(k, carry):
        flux_copy(me, lax.rem(me + k, tiles), k).start()
        return carry

    lax.fori_loop(1, tiles, push, 0)

    @pl.when(me < tiles - 1)
    def _():
        lat_copy(0, after).start()
        halo_copy(0, after).start()

    @pl.when(me > 0)
    def _():
        lat_copy(1, before).start()
        halo_copy(1, before).start()

    @pl.when(me == 0)
    def _():
        lat_near[0] = jnp.zeros_like(lat_own)

    @pl.when(me == tiles - 1)
    def _():
        lat_near[1] = jnp.zeros_like(lat_own)

    block = max(nlat, 128)
    group = block // nlat
    span = WINDOW * nflux
    low = me * band - band - 1
    row_id = lax.broadcasted_iota(jnp.int32, (span, block), 0)
    lane_id = lax.broadcasted_iota(jnp.int32, (span, block), 1)
    wanted = low + row_id // nflux
    picks = [
        ((lane_id == wanted + h * nlat) & (wanted >= 0) & (wanted < nlat))
        .astype(jnp.float32).astype(jnp.bfloat16)
        for h in range(group)
    ]
    pairs = tiles * nflux
    same_flux = (
        lax.broadcasted_iota(jnp.int32, (span, pairs), 0) % nflux
        == lax.broadcasted_iota(jnp.int32, (span, pairs), 1) % nflux
    )
    place_row = lax.broadcasted_iota(jnp.int32, (pairs, nlon), 0)
    place_lane = lax.broadcasted_iota(jnp.int32, (pairs, nlon), 1)

    def arrived(k, carry):
        source = lax.rem(me + k, tiles)
        flux_copy(source, source, k).wait_recv()
        return carry

    lax.fori_loop(1, tiles, arrived, 0)

    for copy in local:
        copy.wait()

    cells = jnp.zeros((span, nlon), jnp.float32)
    for number in range(per_dev):
        start = number // group * block
        piece = sectors[:, :, start : start + block].reshape(pairs, block)
        found = lax.dot_general(
            picks[number % group], piece, (((1,), (1,)), ((), ())),
            preferred_element_type=jnp.float32,
        )
        found = jnp.where(same_flux, found, 0.0).astype(jnp.bfloat16)
        place = (
            (place_lane == place_row // nflux * per_dev + number)
            .astype(jnp.float32).astype(jnp.bfloat16)
        )
        cells = cells + jnp.dot(found, place, preferred_element_type=jnp.float32)
    across = jnp.dot(
        cells.astype(jnp.bfloat16), lon[...], preferred_element_type=jnp.float32
    )

    @pl.when(me > 0)
    def _():
        lat_copy(0, before).wait_recv()

    @pl.when(me < tiles - 1)
    def _():
        lat_copy(1, after).wait_recv()

    weights = [(lat_near[0], rows - HALO + r, 0) for r in range(HALO)]
    weights += [(lat_own[...], r, band) for r in range(rows)]
    weights += [(lat_near[1], r, 2 * band) for r in range(HALO)]
    mapped = []
    for table, r, offset in weights:
        total = None
        for a in range(taps):
            level = (offset + a) * nflux
            term = table[a : a + 1, r : r + 1] * across[level : level + nflux]
            total = term if total is None else total + term
        mapped.append(total)
    q_out[...] = jnp.concatenate(mapped, axis=0).astype(jnp.bfloat16)

    @pl.when(me > 0)
    def _():
        halo_copy(0, before).wait_recv()
        halo_copy(1, before).wait_send()
        lat_copy(1, before).wait_send()

    @pl.when(me < tiles - 1)
    def _():
        halo_copy(1, after).wait_recv()
        halo_copy(0, after).wait_send()
        lat_copy(0, after).wait_send()

    def left(k, carry):
        flux_copy(me, lax.rem(me + k, tiles), k).wait_send()
        return carry

    lax.fori_loop(1, tiles, left, 0)


def gelu(y):
    return 0.5 * y * (1.0 + lax.erf(y * 0.7071067811865476))


def ocean_kernel(
    tiles, ocean, halo, q, proj, kernel, bias, head, next_out, fields_out,
    raw, state, hidden, taps, result, in_sem, out_sem,
):
    me = lax.axis_index("tile")
    rows, width, chans = ocean.shape
    nflux = proj.shape[0]
    layers = kernel.shape[0]
    pairs = rows // 2
    nfields = head.shape[0]
    wide = 3 * chans

    def fetch(p):
        return pltpu.make_async_copy(
            ocean.at[pl.ds(2 * p - 2, 2)], raw.at[pl.ds(2 * p, 2)], in_sem.at[p]
        )

    def fetch_halo(slot):
        p = slot * (pairs + 1)
        return pltpu.make_async_copy(
            halo.at[pl.ds(slot * HALO, HALO)], raw.at[pl.ds(2 * p, 2)], in_sem.at[p]
        )

    fetch_halo(0).start()
    for p in range(1, pairs + 1):
        fetch(p).start()
    fetch_halo(1).start()

    zero = jnp.zeros((chans, chans), jnp.bfloat16)
    for layer in range(layers):
        for i in range(4):
            for o in range(2):
                for dx in range(3):
                    dy = i - o
                    tap = kernel[layer, 3 * dy + dx] if 0 <= dy < 3 else zero
                    taps[
                        layer, i * wide + dx * chans : i * wide + (dx + 1) * chans,
                        o * chans : (o + 1) * chans,
                    ] = tap

    spread = jnp.concatenate([proj[...].astype(jnp.float32)] * 2, axis=0)
    spread = jnp.concatenate([spread] * 2, axis=1)
    spread = jnp.where(
        lax.broadcasted_iota(jnp.int32, spread.shape, 0) // nflux
        == lax.broadcasted_iota(jnp.int32, spread.shape, 1) // chans,
        spread, 0.0,
    ).astype(jnp.bfloat16)

    def put(ref, p, o, value):
        lane = o * wide
        ref[p, :, lane : lane + chans] = pltpu.roll(value, 1, 0).astype(jnp.bfloat16)
        ref[p, :, lane + 2 * chans : lane + wide] = pltpu.roll(value, width - 1, 0).astype(
            jnp.bfloat16
        )

    def force(p):
        pltpu.make_async_copy(
            halo.at[pl.ds(0, 2)], raw.at[pl.ds(2 * p, 2)], in_sem.at[p]
        ).wait()
        forcing = lax.dot_general(
            q[pl.ds(pl.multiple_of(p * 2 * nflux, 2 * nflux), 2 * nflux), :], spread,
            (((0,), (0,)), ((), ())), preferred_element_type=jnp.float32,
        )
        for o in range(2):
            u = raw[2 * p + o].astype(jnp.float32) + forcing[:, o * chans : (o + 1) * chans]
            u = u.astype(jnp.bfloat16)
            state[p, :, o * wide + chans : o * wide + 2 * chans] = u
            put(state, p, o, u.astype(jnp.float32))

    def conv(source, j, layer, n):
        near = source[pl.ds(j, n)].reshape(n * width, 2 * wide)
        far = source[pl.ds(j + 1, n)].reshape(n * width, 2 * wide)
        y = jnp.dot(
            jnp.concatenate([near, far], axis=1), taps[layer], preferred_element_type=jnp.float32
        )
        b = bias[layer : layer + 1, :]
        g0 = gelu(y[:, :chans] + b)
        g1 = gelu(y[:, chans:] + b)
        v0 = near[:, wide + chans : wide + 2 * chans].astype(jnp.float32) + g0
        v1 = far[:, chans : 2 * chans].astype(jnp.float32) + g1
        return v0.astype(jnp.bfloat16).reshape(n, width, chans), v1.astype(jnp.bfloat16).reshape(n, width, chans)

    def first(j, n):
        for o, v in enumerate(conv(state, j, 0, n)):
            lane = o * wide + chans
            for i in range(n):
                hidden[j + i, :, lane : lane + chans] = v[i]
                put(hidden, j + i, o, v[i].astype(jnp.float32))

    def store(m):
        return pltpu.make_async_copy(
            result.at[pl.ds(2 * m, 2)], next_out.at[pl.ds(2 * m, 2)], out_sem.at[m]
        )

    def second(m, n):
        for o, v in enumerate(conv(hidden, m, 1, n)):
            for i in range(n):
                result[2 * m + 2 * i + o] = v[i]
                fields_out[:, 2 * m + 2 * i + o, :] = lax.dot_general(
                    head[...], v[i], (((1,), (1,)), ((), ())), preferred_element_type=jnp.float32
                )
        for i in range(n):
            store(m + i).start()

    pl.loop(0, pairs + 2)(force)

    @pl.when(me == 0)
    def _():
        state[0] = jnp.zeros((width, 2 * wide), jnp.bfloat16)

    @pl.when(me == tiles - 1)
    def _():
        state[pairs + 1] = jnp.zeros((width, 2 * wide), jnp.bfloat16)

    first(0, pairs + 1)

    @pl.when(me == 0)
    def _():
        hidden[0, :, :wide] = jnp.zeros((width, wide), jnp.bfloat16)

    @pl.when(me == tiles - 1)
    def _():
        hidden[pairs, :, wide:] = jnp.zeros((width, wide), jnp.bfloat16)

    half = pairs // 2

    @pl.loop(0, 2)
    def _(j):
        second(half * j, half)

    def finish(m, carry):
        store(m).wait()
        return carry

    lax.fori_loop(0, pairs, finish, 0)


def ocean_step(tiles, ocean, halo, q, proj, kernel, bias, head):
    rows, width, chans = ocean.shape
    vmem = pl.BlockSpec(memory_space=pltpu.VMEM)
    hbm = pl.BlockSpec(memory_space=pltpu.HBM)
    pairs = rows // 2
    wide = 3 * chans
    return pl.pallas_call(
        functools.partial(ocean_kernel, tiles),
        out_shape=(
            jax.ShapeDtypeStruct(ocean.shape, jnp.bfloat16),
            jax.ShapeDtypeStruct((head.shape[1], rows, width), jnp.float32),
        ),
        in_specs=[hbm, hbm, vmem, vmem, vmem, vmem, vmem],
        out_specs=(hbm, vmem),
        scratch_shapes=[
            pltpu.VMEM((rows + 2 * HALO, width, chans), jnp.bfloat16),
            pltpu.VMEM((pairs + 2, width, 2 * wide), jnp.bfloat16),
            pltpu.VMEM((pairs + 1, width, 2 * wide), jnp.bfloat16),
            pltpu.VMEM((kernel.shape[0], 4 * wide, 2 * chans), jnp.bfloat16),
            pltpu.VMEM(ocean.shape, jnp.bfloat16),
            pltpu.SemaphoreType.DMA((pairs + 2,)),
            pltpu.SemaphoreType.DMA((pairs,)),
        ],
        compiler_params=pltpu.CompilerParams(vmem_limit_bytes=60 * 2**20),
        name="ocean",
    )(ocean, halo, q, proj, kernel, bias, head.T)


def shards(
    ocean_state, atm_flux, lat_weights, lon_weights, flux_proj, conv_kernel, conv_bias, head
):
    rows, width, chans = ocean_state.shape
    tiles = lax.axis_size("tile")
    nflux = atm_flux.shape[0]
    vmem = pl.BlockSpec(memory_space=pltpu.VMEM)
    hbm = pl.BlockSpec(memory_space=pltpu.HBM)
    pair_sem = pltpu.SemaphoreType.DMA((2,))
    q, halo = pl.pallas_call(
        functools.partial(exchange_kernel, tiles),
        out_shape=(
            jax.ShapeDtypeStruct(((rows + 2 * HALO) * nflux, width), jnp.bfloat16),
            jax.ShapeDtypeStruct((2 * HALO, width, chans), jnp.bfloat16),
        ),
        in_specs=[hbm, hbm, hbm, hbm],
        out_specs=(vmem, hbm),
        scratch_shapes=[
            pltpu.VMEM((tiles,) + atm_flux.shape, jnp.bfloat16),
            pltpu.VMEM((2,) + lat_weights.shape[::-1], jnp.float32),
            pltpu.VMEM(lat_weights.shape[::-1], jnp.float32),
            pltpu.VMEM(lon_weights.shape, jnp.bfloat16),
            pltpu.SemaphoreType.DMA((tiles,)),
            pltpu.SemaphoreType.DMA((tiles,)),
            pair_sem, pair_sem, pair_sem, pair_sem,
            pltpu.SemaphoreType.DMA((3,)),
        ],
        compiler_params=pltpu.CompilerParams(
            collective_id=0, has_side_effects=True, vmem_limit_bytes=60 * 2**20
        ),
        name="exchange",
    )(ocean_state, atm_flux, lat_weights.T, lon_weights)
    return ocean_step(
        tiles, ocean_state, halo, q, flux_proj, conv_kernel, conv_bias, head
    )


def solution(mesh):
    in_specs = (
        P(("ens", "tile"), None, None),
        P(None, ("ens", "tile")),
        P("tile", None),
        P(),
        P(),
        P(),
        P(),
        P(),
    )
    out_specs = (P(("ens", "tile"), None, None), P(None, ("ens", "tile"), None))
    return jax.shard_map(shards, mesh=mesh, in_specs=in_specs, out_specs=out_specs, check_vma=False)
```

```python
import functools

import jax
import jax.numpy as jnp
from jax import lax
from jax.experimental import pallas as pl
from jax.experimental.pallas import tpu as pltpu
from jax.sharding import PartitionSpec as P

MESH = pl.DeviceIdType.MESH
HALO = 2
WINDOW = 16


def exchange_kernel(
    tiles, ocean, flux_in, lat_in, lon_in, q_out, halo_out,
    flux, parcels, sectors, lat_near, lat_own, lon, send, recv, halo_send, halo_recv, lat_send, lat_recv,
    local_sem,
):
    me = lax.axis_index("tile")
    rows, width, _ = ocean.shape
    nflux = flux_in.shape[0]
    nlon = lon_in.shape[0]
    per_dev = nlon // tiles
    nlat = flux_in.shape[1] // per_dev
    band = nlat // tiles
    taps = lat_in.shape[0]

    barrier = pltpu.get_barrier_semaphore()
    local = [
        pltpu.make_async_copy(flux_in, flux, local_sem.at[0]),
        pltpu.make_async_copy(lat_in, lat_own, local_sem.at[1]),
        pltpu.make_async_copy(lon_in, lon, local_sem.at[2]),
    ]
    for copy in local:
        copy.start()

    def greet(k, carry):
        pl.semaphore_signal(
            barrier, inc=1, device_id={"tile": lax.rem(me + k, tiles)}, device_id_type=MESH
        )
        return carry

    lax.fori_loop(1, tiles, greet, 0)
    local[0].wait()
    block = per_dev * WINDOW
    cell = lax.broadcasted_iota(jnp.int32, (flux.shape[1], block), 0)
    slot_lane = lax.broadcasted_iota(jnp.int32, (flux.shape[1], block), 1)
    gap = jnp.where(
        cell // nlat == slot_lane // WINDOW, cell % nlat - slot_lane % WINDOW, -2 * nlat
    )

    def parcel(target):
        pick = (gap == target * band - band - 1).astype(jnp.float32).astype(jnp.bfloat16)
        parcels[target] = jnp.dot(
            flux[...], pick, preferred_element_type=jnp.float32
        ).astype(jnp.bfloat16)

    pl.loop(0, tiles)(parcel)
    pl.semaphore_wait(barrier, tiles - 1)

    def flux_copy(slot, target, sem):
        return pltpu.make_async_remote_copy(
            src_ref=parcels.at[target], dst_ref=sectors.at[slot], send_sem=send.at[sem], recv_sem=recv.at[slot],
            device_id={"tile": target}, device_id_type=MESH,
        )

    def lat_copy(slot, target):
        return pltpu.make_async_remote_copy(
            src_ref=lat_in, dst_ref=lat_near.at[slot], send_sem=lat_send.at[slot],
            recv_sem=lat_recv.at[slot], device_id={"tile": target}, device_id_type=MESH,
        )

    def halo_copy(slot, target):
        first = rows - HALO if slot == 0 else 0
        return pltpu.make_async_remote_copy(
            src_ref=ocean.at[pl.ds(first, HALO)], dst_ref=halo_out.at[pl.ds(slot * HALO, HALO)],
            send_sem=halo_send.at[slot], recv_sem=halo_recv.at[slot],
            device_id={"tile": target}, device_id_type=MESH,
        )

    after = lax.rem(me + 1, tiles)
    before = lax.rem(me + tiles - 1, tiles)

    def push(k, carry):
        flux_copy(me, lax.rem(me + k, tiles), k).start()
        return carry

    lax.fori_loop(1, tiles, push, 0)

    @pl.when(me < tiles - 1)
    def _():
        lat_copy(0, after).start()
        halo_copy(0, after).start()

    @pl.when(me > 0)
    def _():
        lat_copy(1, before).start()
        halo_copy(1, before).start()

    @pl.when(me == 0)
    def _():
        lat_near[0] = jnp.zeros_like(lat_own)

    @pl.when(me == tiles - 1)
    def _():
        lat_near[1] = jnp.zeros_like(lat_own)

    sectors[me] = parcels[me]
    span = WINDOW * nflux
    lane_gap = (
        lax.broadcasted_iota(jnp.int32, (span, block), 1)
        - lax.broadcasted_iota(jnp.int32, (span, block), 0) // nflux
    )
    pairs = tiles * nflux
    same_flux = (
        lax.broadcasted_iota(jnp.int32, (span, pairs), 0) % nflux
        == lax.broadcasted_iota(jnp.int32, (span, pairs), 1) % nflux
    )
    place_row = lax.broadcasted_iota(jnp.int32, (pairs, nlon), 0)
    place_lane = lax.broadcasted_iota(jnp.int32, (pairs, nlon), 1)

    def arrived(k, carry):
        source = lax.rem(me + k, tiles)
        flux_copy(source, source, k).wait_recv()
        return carry

    lax.fori_loop(1, tiles, arrived, 0)

    for copy in local[1:]:
        copy.wait()

    arrivals = sectors[...].reshape(pairs, block)
    cells = jnp.zeros((span, nlon), jnp.float32)
    for number in range(per_dev):
        pick = (lane_gap == number * WINDOW).astype(jnp.float32).astype(jnp.bfloat16)
        found = lax.dot_general(
            pick, arrivals, (((1,), (1,)), ((), ())),
            preferred_element_type=jnp.float32,
        )
        found = jnp.where(same_flux, found, 0.0).astype(jnp.bfloat16)
        place = (
            (place_lane == place_row // nflux * per_dev + number)
            .astype(jnp.float32).astype(jnp.bfloat16)
        )
        cells = cells + jnp.dot(found, place, preferred_element_type=jnp.float32)
    across = jnp.dot(
        cells.astype(jnp.bfloat16), lon[...], preferred_element_type=jnp.float32
    )

    @pl.when(me > 0)
    def _():
        lat_copy(0, before).wait_recv()

    @pl.when(me < tiles - 1)
    def _():
        lat_copy(1, after).wait_recv()

    weights = [(lat_near[0], rows - HALO + r, 0) for r in range(HALO)]
    weights += [(lat_own[...], r, band) for r in range(rows)]
    weights += [(lat_near[1], r, 2 * band) for r in range(HALO)]
    mapped = []
    for table, r, offset in weights:
        total = None
        for a in range(taps):
            level = (offset + a) * nflux
            term = table[a : a + 1, r : r + 1] * across[level : level + nflux]
            total = term if total is None else total + term
        mapped.append(total)
    q_out[...] = jnp.concatenate(mapped, axis=0).astype(jnp.bfloat16)

    @pl.when(me > 0)
    def _():
        halo_copy(0, before).wait_recv()
        halo_copy(1, before).wait_send()
        lat_copy(1, before).wait_send()

    @pl.when(me < tiles - 1)
    def _():
        halo_copy(1, after).wait_recv()
        halo_copy(0, after).wait_send()
        lat_copy(0, after).wait_send()

    def left(k, carry):
        flux_copy(me, lax.rem(me + k, tiles), k).wait_send()
        return carry

    lax.fori_loop(1, tiles, left, 0)


def gelu(y):
    return 0.5 * y * (1.0 + lax.erf(y * 0.7071067811865476))


def ocean_kernel(
    tiles, ocean, halo, q, proj, kernel, bias, head, next_out, fields_out,
    raw, state, hidden, taps, result, in_sem, out_sem,
):
    me = lax.axis_index("tile")
    rows, width, chans = ocean.shape
    nflux = proj.shape[0]
    layers = kernel.shape[0]
    pairs = rows // 2
    nfields = head.shape[0]
    wide = 3 * chans

    def fetch(p):
        return pltpu.make_async_copy(
            ocean.at[pl.ds(2 * p - 2, 2)], raw.at[pl.ds(2 * p, 2)], in_sem.at[p]
        )

    def fetch_halo(slot):
        p = slot * (pairs + 1)
        return pltpu.make_async_copy(
            halo.at[pl.ds(slot * HALO, HALO)], raw.at[pl.ds(2 * p, 2)], in_sem.at[p]
        )

    fetch_halo(0).start()
    for p in range(1, pairs + 1):
        fetch(p).start()
    fetch_halo(1).start()

    zero = jnp.zeros((chans, chans), jnp.bfloat16)
    for layer in range(layers):
        for i in range(4):
            for o in range(2):
                for dx in range(3):
                    dy = i - o
                    tap = kernel[layer, 3 * dy + dx] if 0 <= dy < 3 else zero
                    taps[
                        layer, i * wide + dx * chans : i * wide + (dx + 1) * chans,
                        o * chans : (o + 1) * chans,
                    ] = tap

    spread = jnp.concatenate([proj[...].astype(jnp.float32)] * 2, axis=0)
    spread = jnp.concatenate([spread] * 2, axis=1)
    spread = jnp.where(
        lax.broadcasted_iota(jnp.int32, spread.shape, 0) // nflux
        == lax.broadcasted_iota(jnp.int32, spread.shape, 1) // chans,
        spread, 0.0,
    ).astype(jnp.bfloat16)

    def put(ref, p, o, value):
        lane = o * wide
        ref[p, :, lane : lane + chans] = pltpu.roll(value, 1, 0).astype(jnp.bfloat16)
        ref[p, :, lane + 2 * chans : lane + wide] = pltpu.roll(value, width - 1, 0).astype(
            jnp.bfloat16
        )

    def force(p):
        forcing = lax.dot_general(
            q[pl.ds(p * 2 * nflux, 2 * nflux), :], spread,
            (((0,), (0,)), ((), ())), preferred_element_type=jnp.float32,
        )
        for o in range(2):
            u = raw[2 * p + o].astype(jnp.float32) + forcing[:, o * chans : (o + 1) * chans]
            u = u.astype(jnp.bfloat16)
            state[p, :, o * wide + chans : o * wide + 2 * chans] = u
            put(state, p, o, u.astype(jnp.float32))

    def conv(source, j, layer, n):
        near = source[pl.ds(j, n)].reshape(n * width, 2 * wide)
        far = source[pl.ds(j + 1, n)].reshape(n * width, 2 * wide)
        y = jnp.dot(
            jnp.concatenate([near, far], axis=1), taps[layer], preferred_element_type=jnp.float32
        )
        b = bias[layer : layer + 1, :]
        g0 = gelu(y[:, :chans] + b)
        g1 = gelu(y[:, chans:] + b)
        v0 = near[:, wide + chans : wide + 2 * chans].astype(jnp.float32) + g0
        v1 = far[:, chans : 2 * chans].astype(jnp.float32) + g1
        return v0.astype(jnp.bfloat16).reshape(n, width, chans), v1.astype(jnp.bfloat16).reshape(n, width, chans)

    def first(j, n):
        for o, v in enumerate(conv(state, j, 0, n)):
            lane = o * wide + chans
            for i in range(n):
                hidden[j + i, :, lane : lane + chans] = v[i]
                put(hidden, j + i, o, v[i].astype(jnp.float32))

    def store(m):
        return pltpu.make_async_copy(
            result.at[pl.ds(2 * m, 2)], next_out.at[pl.ds(2 * m, 2)], out_sem.at[m]
        )

    def second(m, n):
        for o, v in enumerate(conv(hidden, m, 1, n)):
            for i in range(n):
                result[2 * m + 2 * i + o] = v[i]
                fields_out[:, 2 * m + 2 * i + o, :] = lax.dot_general(
                    head[...], v[i], (((1,), (1,)), ((), ())), preferred_element_type=jnp.float32
                )
        for i in range(n):
            store(m + i).start()

    for p in range(pairs + 2):
        pltpu.make_async_copy(
            halo.at[pl.ds(0, 2)], raw.at[pl.ds(2 * p, 2)], in_sem.at[p]
        ).wait()
    for p in range(pairs + 2):
        force(p)

    @pl.when(me == 0)
    def _():
        state[0] = jnp.zeros((width, 2 * wide), jnp.bfloat16)

    @pl.when(me == tiles - 1)
    def _():
        state[pairs + 1] = jnp.zeros((width, 2 * wide), jnp.bfloat16)

    first(0, pairs + 1)

    @pl.when(me == 0)
    def _():
        hidden[0, :, :wide] = jnp.zeros((width, wide), jnp.bfloat16)

    @pl.when(me == tiles - 1)
    def _():
        hidden[pairs, :, wide:] = jnp.zeros((width, wide), jnp.bfloat16)

    half = pairs // 2

    @pl.loop(0, 2)
    def _(j):
        second(half * j, half)

    def finish(m, carry):
        store(m).wait()
        return carry

    lax.fori_loop(0, pairs, finish, 0)


def ocean_step(tiles, ocean, halo, q, proj, kernel, bias, head):
    rows, width, chans = ocean.shape
    vmem = pl.BlockSpec(memory_space=pltpu.VMEM)
    hbm = pl.BlockSpec(memory_space=pltpu.HBM)
    pairs = rows // 2
    wide = 3 * chans
    return pl.pallas_call(
        functools.partial(ocean_kernel, tiles),
        out_shape=(
            jax.ShapeDtypeStruct(ocean.shape, jnp.bfloat16),
            jax.ShapeDtypeStruct((head.shape[1], rows, width), jnp.float32),
        ),
        in_specs=[hbm, hbm, vmem, vmem, vmem, vmem, vmem],
        out_specs=(hbm, vmem),
        scratch_shapes=[
            pltpu.VMEM((rows + 2 * HALO, width, chans), jnp.bfloat16),
            pltpu.VMEM((pairs + 2, width, 2 * wide), jnp.bfloat16),
            pltpu.VMEM((pairs + 1, width, 2 * wide), jnp.bfloat16),
            pltpu.VMEM((kernel.shape[0], 4 * wide, 2 * chans), jnp.bfloat16),
            pltpu.VMEM(ocean.shape, jnp.bfloat16),
            pltpu.SemaphoreType.DMA((pairs + 2,)),
            pltpu.SemaphoreType.DMA((pairs,)),
        ],
        compiler_params=pltpu.CompilerParams(vmem_limit_bytes=60 * 2**20),
        name="ocean",
    )(ocean, halo, q, proj, kernel, bias, head.T)


def shards(
    ocean_state, atm_flux, lat_weights, lon_weights, flux_proj, conv_kernel, conv_bias, head
):
    rows, width, chans = ocean_state.shape
    tiles = lax.axis_size("tile")
    nflux = atm_flux.shape[0]
    vmem = pl.BlockSpec(memory_space=pltpu.VMEM)
    hbm = pl.BlockSpec(memory_space=pltpu.HBM)
    parcel = lon_weights.shape[0] // tiles * WINDOW
    pair_sem = pltpu.SemaphoreType.DMA((2,))
    q, halo = pl.pallas_call(
        functools.partial(exchange_kernel, tiles),
        out_shape=(
            jax.ShapeDtypeStruct(((rows + 2 * HALO) * nflux, width), jnp.bfloat16),
            jax.ShapeDtypeStruct((2 * HALO, width, chans), jnp.bfloat16),
        ),
        in_specs=[hbm, hbm, hbm, hbm],
        out_specs=(vmem, hbm),
        scratch_shapes=[
            pltpu.VMEM(atm_flux.shape, jnp.bfloat16),
            pltpu.VMEM((tiles, nflux, parcel), jnp.bfloat16),
            pltpu.VMEM((tiles, nflux, parcel), jnp.bfloat16),
            pltpu.VMEM((2,) + lat_weights.shape[::-1], jnp.float32),
            pltpu.VMEM(lat_weights.shape[::-1], jnp.float32),
            pltpu.VMEM(lon_weights.shape, jnp.bfloat16),
            pltpu.SemaphoreType.DMA((tiles,)),
            pltpu.SemaphoreType.DMA((tiles,)),
            pair_sem, pair_sem, pair_sem, pair_sem,
            pltpu.SemaphoreType.DMA((3,)),
        ],
        compiler_params=pltpu.CompilerParams(
            collective_id=0, has_side_effects=True, vmem_limit_bytes=60 * 2**20
        ),
        name="exchange",
    )(ocean_state, atm_flux, lat_weights.T, lon_weights)
    return ocean_step(
        tiles, ocean_state, halo, q, flux_proj, conv_kernel, conv_bias, head
    )


def solution(mesh):
    in_specs = (
        P(("ens", "tile"), None, None),
        P(None, ("ens", "tile")),
        P("tile", None),
        P(),
        P(),
        P(),
        P(),
        P(),
    )
    out_specs = (P(("ens", "tile"), None, None), P(None, ("ens", "tile"), None))
    return jax.shard_map(shards, mesh=mesh, in_specs=in_specs, out_specs=out_specs, check_vma=False)
```

```python
import functools

import jax
import jax.numpy as jnp
from jax import lax
from jax.experimental import pallas as pl
from jax.experimental.pallas import tpu as pltpu
from jax.sharding import PartitionSpec as P

MESH = pl.DeviceIdType.MESH
HALO = 2
WINDOW = 16


def exchange_kernel(
    tiles, ocean, flux_in, lat_in, lon_in, q_out, halo_out,
    flux, parcels, sectors, lat_near, lat_own, lon, send, recv, halo_send, halo_recv, lat_send, lat_recv,
    local_sem,
):
    me = lax.axis_index("tile")
    rows, width, _ = ocean.shape
    nflux = flux_in.shape[0]
    nlon = lon_in.shape[0]
    per_dev = nlon // tiles
    nlat = flux_in.shape[1] // per_dev
    band = nlat // tiles
    taps = lat_in.shape[0]

    barrier = pltpu.get_barrier_semaphore()
    local = [
        pltpu.make_async_copy(flux_in, flux, local_sem.at[0]),
        pltpu.make_async_copy(lat_in, lat_own, local_sem.at[1]),
        pltpu.make_async_copy(lon_in, lon, local_sem.at[2]),
    ]
    for copy in local:
        copy.start()

    def greet(k, carry):
        pl.semaphore_signal(
            barrier, inc=1, device_id={"tile": lax.rem(me + k, tiles)}, device_id_type=MESH
        )
        return carry

    lax.fori_loop(1, tiles, greet, 0)
    local[0].wait()
    block = per_dev * WINDOW
    cell = lax.broadcasted_iota(jnp.int32, (flux.shape[1], block), 0)
    slot_lane = lax.broadcasted_iota(jnp.int32, (flux.shape[1], block), 1)
    gap = jnp.where(
        cell // nlat == slot_lane // WINDOW, cell % nlat - slot_lane % WINDOW, -2 * nlat
    )

    def parcel(target):
        pick = (gap == target * band - band - 1).astype(jnp.float32).astype(jnp.bfloat16)
        parcels[target] = jnp.dot(
            flux[...], pick, preferred_element_type=jnp.float32
        ).astype(jnp.bfloat16)

    pl.loop(0, tiles)(parcel)
    pl.semaphore_wait(barrier, tiles - 1)

    def flux_copy(slot, target, sem):
        return pltpu.make_async_remote_copy(
            src_ref=parcels.at[target], dst_ref=sectors.at[slot], send_sem=send.at[sem], recv_sem=recv.at[slot],
            device_id={"tile": target}, device_id_type=MESH,
        )

    def lat_copy(slot, target):
        return pltpu.make_async_remote_copy(
            src_ref=lat_in, dst_ref=lat_near.at[slot], send_sem=lat_send.at[slot],
            recv_sem=lat_recv.at[slot], device_id={"tile": target}, device_id_type=MESH,
        )

    def halo_copy(slot, target):
        first = rows - HALO if slot == 0 else 0
        return pltpu.make_async_remote_copy(
            src_ref=ocean.at[pl.ds(first, HALO)], dst_ref=halo_out.at[pl.ds(slot * HALO, HALO)],
            send_sem=halo_send.at[slot], recv_sem=halo_recv.at[slot],
            device_id={"tile": target}, device_id_type=MESH,
        )

    after = lax.rem(me + 1, tiles)
    before = lax.rem(me + tiles - 1, tiles)

    def push(k, carry):
        flux_copy(me, lax.rem(me + k, tiles), k).start()
        return carry

    @pl.when(me < tiles - 1)
    def _():
        lat_copy(0, after).start()
        halo_copy(0, after).start()

    @pl.when(me > 0)
    def _():
        lat_copy(1, before).start()
        halo_copy(1, before).start()

    lax.fori_loop(1, tiles, push, 0)

    @pl.when(me == 0)
    def _():
        lat_near[0] = jnp.zeros_like(lat_own)

    @pl.when(me == tiles - 1)
    def _():
        lat_near[1] = jnp.zeros_like(lat_own)

    sectors[me] = parcels[me]
    span = WINDOW * nflux
    lane_gap = (
        lax.broadcasted_iota(jnp.int32, (span, block), 1)
        - lax.broadcasted_iota(jnp.int32, (span, block), 0) // nflux
    )
    pairs = tiles * nflux
    same_flux = (
        lax.broadcasted_iota(jnp.int32, (span, pairs), 0) % nflux
        == lax.broadcasted_iota(jnp.int32, (span, pairs), 1) % nflux
    )
    place_row = lax.broadcasted_iota(jnp.int32, (pairs, nlon), 0)
    place_lane = lax.broadcasted_iota(jnp.int32, (pairs, nlon), 1)

    def arrived(k, carry):
        source = lax.rem(me + k, tiles)
        flux_copy(source, source, k).wait_recv()
        return carry

    lax.fori_loop(1, tiles, arrived, 0)

    for copy in local[1:]:
        copy.wait()

    arrivals = sectors[...].reshape(pairs, block)
    cells = jnp.zeros((span, nlon), jnp.float32)
    for number in range(per_dev):
        pick = (lane_gap == number * WINDOW).astype(jnp.float32).astype(jnp.bfloat16)
        found = lax.dot_general(
            pick, arrivals, (((1,), (1,)), ((), ())),
            preferred_element_type=jnp.float32,
        )
        found = jnp.where(same_flux, found, 0.0).astype(jnp.bfloat16)
        place = (
            (place_lane == place_row // nflux * per_dev + number)
            .astype(jnp.float32).astype(jnp.bfloat16)
        )
        cells = cells + jnp.dot(found, place, preferred_element_type=jnp.float32)
    across = jnp.dot(
        cells.astype(jnp.bfloat16), lon[...], preferred_element_type=jnp.float32
    )

    @pl.when(me > 0)
    def _():
        lat_copy(0, before).wait_recv()

    @pl.when(me < tiles - 1)
    def _():
        lat_copy(1, after).wait_recv()

    weights = [(lat_near[0], rows - HALO + r, 0) for r in range(HALO)]
    weights += [(lat_own[...], r, band) for r in range(rows)]
    weights += [(lat_near[1], r, 2 * band) for r in range(HALO)]
    mapped = []
    for table, r, offset in weights:
        total = None
        for a in range(taps):
            level = (offset + a) * nflux
            term = table[a : a + 1, r : r + 1] * across[level : level + nflux]
            total = term if total is None else total + term
        mapped.append(total)
    q_out[...] = jnp.concatenate(mapped, axis=0).astype(jnp.bfloat16)

    @pl.when(me > 0)
    def _():
        halo_copy(0, before).wait_recv()
        halo_copy(1, before).wait_send()
        lat_copy(1, before).wait_send()

    @pl.when(me < tiles - 1)
    def _():
        halo_copy(1, after).wait_recv()
        halo_copy(0, after).wait_send()
        lat_copy(0, after).wait_send()

    def left(k, carry):
        flux_copy(me, lax.rem(me + k, tiles), k).wait_send()
        return carry

    lax.fori_loop(1, tiles, left, 0)


def gelu(y):
    return 0.5 * y * (1.0 + lax.erf(y * 0.7071067811865476))


def ocean_kernel(
    tiles, ocean, halo, q, proj, kernel, bias, head, next_out, fields_out,
    raw, state, hidden, taps, result, in_sem, out_sem,
):
    me = lax.axis_index("tile")
    rows, width, chans = ocean.shape
    nflux = proj.shape[0]
    layers = kernel.shape[0]
    pairs = rows // 2
    nfields = head.shape[0]
    wide = 3 * chans

    def fetch(p):
        return pltpu.make_async_copy(
            ocean.at[pl.ds(2 * p - 2, 2)], raw.at[pl.ds(2 * p, 2)], in_sem.at[p]
        )

    def fetch_halo(slot):
        p = slot * (pairs + 1)
        return pltpu.make_async_copy(
            halo.at[pl.ds(slot * HALO, HALO)], raw.at[pl.ds(2 * p, 2)], in_sem.at[p]
        )

    fetch_halo(0).start()
    for p in range(1, pairs + 1):
        fetch(p).start()
    fetch_halo(1).start()

    zero = jnp.zeros((chans, chans), jnp.bfloat16)
    for layer in range(layers):
        for i in range(4):
            for o in range(2):
                for dx in range(3):
                    dy = i - o
                    tap = kernel[layer, 3 * dy + dx] if 0 <= dy < 3 else zero
                    taps[
                        layer, i * wide + dx * chans : i * wide + (dx + 1) * chans,
                        o * chans : (o + 1) * chans,
                    ] = tap

    spread = jnp.concatenate([proj[...].astype(jnp.float32)] * 2, axis=0)
    spread = jnp.concatenate([spread] * 2, axis=1)
    spread = jnp.where(
        lax.broadcasted_iota(jnp.int32, spread.shape, 0) // nflux
        == lax.broadcasted_iota(jnp.int32, spread.shape, 1) // chans,
        spread, 0.0,
    ).astype(jnp.bfloat16)

    def put(ref, p, o, value):
        lane = o * wide
        ref[p, :, lane : lane + chans] = pltpu.roll(value, 1, 0).astype(jnp.bfloat16)
        ref[p, :, lane + 2 * chans : lane + wide] = pltpu.roll(value, width - 1, 0).astype(
            jnp.bfloat16
        )

    def force(p):
        forcing = lax.dot_general(
            q[pl.ds(p * 2 * nflux, 2 * nflux), :], spread,
            (((0,), (0,)), ((), ())), preferred_element_type=jnp.float32,
        )
        for o in range(2):
            u = raw[2 * p + o].astype(jnp.float32) + forcing[:, o * chans : (o + 1) * chans]
            u = u.astype(jnp.bfloat16)
            state[p, :, o * wide + chans : o * wide + 2 * chans] = u
            put(state, p, o, u.astype(jnp.float32))

    def conv(source, j, layer, n):
        near = source[pl.ds(j, n)].reshape(n * width, 2 * wide)
        far = source[pl.ds(j + 1, n)].reshape(n * width, 2 * wide)
        y = jnp.dot(
            jnp.concatenate([near, far], axis=1), taps[layer], preferred_element_type=jnp.float32
        )
        b = bias[layer : layer + 1, :]
        g0 = gelu(y[:, :chans] + b)
        g1 = gelu(y[:, chans:] + b)
        v0 = near[:, wide + chans : wide + 2 * chans].astype(jnp.float32) + g0
        v1 = far[:, chans : 2 * chans].astype(jnp.float32) + g1
        return v0.astype(jnp.bfloat16).reshape(n, width, chans), v1.astype(jnp.bfloat16).reshape(n, width, chans)

    def first(j, n):
        for o, v in enumerate(conv(state, j, 0, n)):
            lane = o * wide + chans
            for i in range(n):
                hidden[j + i, :, lane : lane + chans] = v[i]
                put(hidden, j + i, o, v[i].astype(jnp.float32))

    def store(m):
        return pltpu.make_async_copy(
            result.at[pl.ds(2 * m, 2)], next_out.at[pl.ds(2 * m, 2)], out_sem.at[m]
        )

    def second(m, n):
        for o, v in enumerate(conv(hidden, m, 1, n)):
            for i in range(n):
                result[2 * m + 2 * i + o] = v[i]
                fields_out[:, 2 * m + 2 * i + o, :] = lax.dot_general(
                    head[...], v[i], (((1,), (1,)), ((), ())), preferred_element_type=jnp.float32
                )
        for i in range(n):
            store(m + i).start()

    for p in range(pairs + 2):
        pltpu.make_async_copy(
            halo.at[pl.ds(0, 2)], raw.at[pl.ds(2 * p, 2)], in_sem.at[p]
        ).wait()
    for p in range(pairs + 2):
        force(p)

    @pl.when(me == 0)
    def _():
        state[0] = jnp.zeros((width, 2 * wide), jnp.bfloat16)

    @pl.when(me == tiles - 1)
    def _():
        state[pairs + 1] = jnp.zeros((width, 2 * wide), jnp.bfloat16)

    first(0, pairs + 1)

    @pl.when(me == 0)
    def _():
        hidden[0, :, :wide] = jnp.zeros((width, wide), jnp.bfloat16)

    @pl.when(me == tiles - 1)
    def _():
        hidden[pairs, :, wide:] = jnp.zeros((width, wide), jnp.bfloat16)

    half = pairs // 2

    @pl.loop(0, 2)
    def _(j):
        second(half * j, half)

    def finish(m, carry):
        store(m).wait()
        return carry

    lax.fori_loop(0, pairs, finish, 0)


def ocean_step(tiles, ocean, halo, q, proj, kernel, bias, head):
    rows, width, chans = ocean.shape
    vmem = pl.BlockSpec(memory_space=pltpu.VMEM)
    hbm = pl.BlockSpec(memory_space=pltpu.HBM)
    pairs = rows // 2
    wide = 3 * chans
    return pl.pallas_call(
        functools.partial(ocean_kernel, tiles),
        out_shape=(
            jax.ShapeDtypeStruct(ocean.shape, jnp.bfloat16),
            jax.ShapeDtypeStruct((head.shape[1], rows, width), jnp.float32),
        ),
        in_specs=[hbm, hbm, vmem, vmem, vmem, vmem, vmem],
        out_specs=(hbm, vmem),
        scratch_shapes=[
            pltpu.VMEM((rows + 2 * HALO, width, chans), jnp.bfloat16),
            pltpu.VMEM((pairs + 2, width, 2 * wide), jnp.bfloat16),
            pltpu.VMEM((pairs + 1, width, 2 * wide), jnp.bfloat16),
            pltpu.VMEM((kernel.shape[0], 4 * wide, 2 * chans), jnp.bfloat16),
            pltpu.VMEM(ocean.shape, jnp.bfloat16),
            pltpu.SemaphoreType.DMA((pairs + 2,)),
            pltpu.SemaphoreType.DMA((pairs,)),
        ],
        compiler_params=pltpu.CompilerParams(vmem_limit_bytes=60 * 2**20),
        name="ocean",
    )(ocean, halo, q, proj, kernel, bias, head.T)


def shards(
    ocean_state, atm_flux, lat_weights, lon_weights, flux_proj, conv_kernel, conv_bias, head
):
    rows, width, chans = ocean_state.shape
    tiles = lax.axis_size("tile")
    nflux = atm_flux.shape[0]
    vmem = pl.BlockSpec(memory_space=pltpu.VMEM)
    hbm = pl.BlockSpec(memory_space=pltpu.HBM)
    parcel = lon_weights.shape[0] // tiles * WINDOW
    pair_sem = pltpu.SemaphoreType.DMA((2,))
    q, halo = pl.pallas_call(
        functools.partial(exchange_kernel, tiles),
        out_shape=(
            jax.ShapeDtypeStruct(((rows + 2 * HALO) * nflux, width), jnp.bfloat16),
            jax.ShapeDtypeStruct((2 * HALO, width, chans), jnp.bfloat16),
        ),
        in_specs=[hbm, hbm, hbm, hbm],
        out_specs=(vmem, hbm),
        scratch_shapes=[
            pltpu.VMEM(atm_flux.shape, jnp.bfloat16),
            pltpu.VMEM((tiles, nflux, parcel), jnp.bfloat16),
            pltpu.VMEM((tiles, nflux, parcel), jnp.bfloat16),
            pltpu.VMEM((2,) + lat_weights.shape[::-1], jnp.float32),
            pltpu.VMEM(lat_weights.shape[::-1], jnp.float32),
            pltpu.VMEM(lon_weights.shape, jnp.bfloat16),
            pltpu.SemaphoreType.DMA((tiles,)),
            pltpu.SemaphoreType.DMA((tiles,)),
            pair_sem, pair_sem, pair_sem, pair_sem,
            pltpu.SemaphoreType.DMA((3,)),
        ],
        compiler_params=pltpu.CompilerParams(
            collective_id=0, has_side_effects=True, vmem_limit_bytes=60 * 2**20
        ),
        name="exchange",
    )(ocean_state, atm_flux, lat_weights.T, lon_weights)
    return ocean_step(
        tiles, ocean_state, halo, q, flux_proj, conv_kernel, conv_bias, head
    )


def solution(mesh):
    in_specs = (
        P(("ens", "tile"), None, None),
        P(None, ("ens", "tile")),
        P("tile", None),
        P(),
        P(),
        P(),
        P(),
        P(),
    )
    out_specs = (P(("ens", "tile"), None, None), P(None, ("ens", "tile"), None))
    return jax.shard_map(shards, mesh=mesh, in_specs=in_specs, out_specs=out_specs, check_vma=False)
```
